32 devices in a mesh: row: 2 (over x), col: 16 (over z, y, core).
Axes of the slice: x: 2, y: 2, z: 4, core: 2. Of those that a mesh axis runs over, the one named last changes fastest.
Arguments:
- inv_anc: float32 [2, 16, 48, 1536], P(None, 'col', None, 'row'), may hold values from -6 to 6, as said below
- factor_cols: float32 [4, 1536, 256], P(None, ('row', 'col')), may hold values from -0.15625 to 0.15625
- couple: float32 [6, 256, 256], replicated, may hold values from -0.1875 to 0.1875
- diag_inv: float32 [4, 256, 256], replicated, may hold values from -6 to 6, as said below
- pattern: int32 [4, 6], replicated, may hold values 0 or 1
- parent: int32 [4], replicated, may hold values from 0 to 4, as said below
Outputs:
- inv_cols: float32 [4, 1536, 256], P(None, ('row', 'col'))
- win_cols: float32 [6, 256, 256], replicated
- win_diag: float32 [4, 256, 256], replicated
The draws below stay inside these ranges and needn't reach their ends.
Inputs may be any that keep to these rules, and one draw needn't show every extreme that they name: parent[0] is 4, meaning a parent in the ancestor set; for j of 1 or more parent[j] is an earlier supernode or 4. The matrix full built from inv_anc as in the reference program is symmetric. Each diag_inv[j] is symmetric.
All inputs are finite; a program needn't handle non-finite values.
Results may differ from the reference program's by a relative error of at most 0.0001.
Values sent between devices are 32-bit elements; how exact they have to be, the bound alone decides.
A program may use at most 64 MiB of HBM per device.

```python
import jax
import jax.numpy as jnp
from jax import lax

W = 256
NSUP = 4
RW = 48
NS = 1536
NB = 6
NPAIR = 6
N_ROW = 2
N_COL = 16


def draw_parent(key, part):
    random_values = jax.random.randint(jax.random.fold_in(key, 37), (NSUP,), 0, 1 << 20)
    positions = jnp.arange(NSUP, dtype=jnp.int32)
    picked = random_values % (positions + 1)
    parent = jnp.where(picked == positions, NSUP, picked)
    parent = parent.at[0].set(NSUP)
    second_free = parent[1] == NSUP
    parent = parent.at[2].set(jnp.where(second_free, 0, parent[2]))
    return parent.astype(jnp.int32)


def symmetric_draw(key, shape):
    raw = jax.random.normal(key, shape, jnp.float32)
    raw = jnp.clip(raw, -4.0, 4.0)
    return (raw + jnp.swapaxes(raw, -1, -2)) * 0.70710678


def draw_inv_anc(key, part):
    full = symmetric_draw(jax.random.fold_in(key, 11), (NS, NS))
    return full.reshape(N_ROW, N_COL, RW, NS).astype(jnp.float32)


def draw_diag_inv(key, part):
    return symmetric_draw(jax.random.fold_in(key, 23), (NSUP, W, W)).astype(jnp.float32)


def touch_ends(result, stream_key, least, top_value):
    index_at = [jax.random.randint(jax.random.fold_in(stream_key, axis), (), 0, length) for axis, length in enumerate(result.shape)]
    widest = result.shape.index(max(result.shape))
    neighbour = index_at[:widest] + [(index_at[widest] + 1) % result.shape[widest]] + index_at[widest + 1:]
    return result.at[tuple(index_at)].set(least).at[tuple(neighbour)].set(top_value)


def levels(stream_key, shape, shards, smallest, largest):
    level, own = 1.0, jax.random.fold_in(stream_key, 6)
    for dim, blocks in shards:
        draws = jnp.exp(jax.random.uniform(jax.random.fold_in(own, dim), (blocks,), jnp.float32, smallest / len(shards), largest / len(shards)))
        level = level * jnp.repeat(draws, shape[dim] // blocks).reshape([-1 if axis == dim else 1 for axis in range(len(shape))])
    return level


def gaussian(own_key, shape, scale, limit, pieces=(), held_as=jnp.bfloat16):
    gain = levels(own_key, shape, pieces, -0.22, 0.18) if pieces else 1.0
    values = jax.random.normal(own_key, shape, jnp.float32) * scale * gain
    return jnp.minimum(jnp.maximum(values, -limit), limit).astype(held_as)


def setup_inputs(seed: int = 0) -> dict:
    splits = jax.random.split(jax.random.key(seed), 7)
    return {
        "inv_anc": draw_inv_anc(jax.random.fold_in(splits[6], 71), 0),
        "factor_cols": gaussian(splits[1], (NSUP, NS, W), NS ** -0.5, 0.15625, ((1, 32),), jnp.float32),
        "couple": gaussian(splits[2], (NPAIR, W, W), (4 * W) ** -0.5, 0.1875, (), jnp.float32),
        "diag_inv": draw_diag_inv(jax.random.fold_in(splits[6], 71), 0),
        "pattern": touch_ends((jax.random.randint(splits[4], (NSUP, NB), 0, 4) < 3).astype(jnp.int32), jax.random.fold_in(splits[4], 1), 0, 1),
        "parent": draw_parent(jax.random.fold_in(splits[6], 71), 0),
    }


exact_mode = lax.Precision.HIGHEST


def product(left, right):
    return jnp.dot(left, right, precision=exact_mode, preferred_element_type=jnp.float32)


def ancestry(parent):
    linked = {}
    for j in range(NSUP):
        for m in range(j):
            linked_now = parent[j] == m
            for p in range(m + 1, j):
                linked_now = linked_now | ((parent[j] == p) & linked[(p, m)])
            linked[(j, m)] = linked_now
    return linked


def couplings(couple, parent):
    linked = ancestry(parent)
    blocks = {}
    for j in range(NSUP):
        for m in range(j):
            blocks[(j, m)] = couple[j * (j - 1) // 2 + m] * linked[(j, m)].astype(jnp.float32)
    return blocks


def window_blocks(crossed, diag_terms, diag_inv, blocks):
    off_diag = {}
    diagonal = []

    def lookup_block(first, second):
        if first == second:
            return diagonal[first]
        if first < second:
            return off_diag[(second, first)]
        return off_diag[(first, second)].T

    for j in range(NSUP):
        for m in range(j):
            running = crossed[(j, m)]
            for q in range(j):
                running = running + product(lookup_block(m, q), blocks[(j, q)])
            off_diag[(j, m)] = -running
        diag_value = diag_inv[j] - diag_terms[j]
        for m in range(j):
            diag_value = diag_value - product(blocks[(j, m)].T, off_diag[(j, m)])
        diagonal.append(diag_value)
    pair_list = [off_diag[(j, m)] for j in range(NSUP) for m in range(j)]
    return jnp.stack(pair_list), jnp.stack(diagonal)


def reference(inv_anc, factor_cols, couple, diag_inv, pattern, parent):
    full_matrix = inv_anc.reshape(NS, NS)
    row_mask = jnp.repeat(pattern.astype(jnp.float32), W, axis=1)
    masked = factor_cols * row_mask[:, :, None]
    blocks = couplings(couple, parent)
    columns = []
    for j in range(NSUP):
        running = product(full_matrix, masked[j])
        for m in range(j):
            running = running + product(columns[m], blocks[(j, m)])
        columns.append(-running)
    crossed = {}
    diag_terms = []
    for j in range(NSUP):
        for m in range(j):
            crossed[(j, m)] = product(columns[m].T, masked[j])
        diag_terms.append(product(masked[j].T, columns[j]))
    pair_blocks, diagonal = window_blocks(crossed, diag_terms, diag_inv, blocks)
    return jnp.stack(columns), pair_blocks, diagonal
```

```python
import jax
import jax.numpy as jnp
from jax import lax
from jax.sharding import PartitionSpec as P


def product(left, right):
    return jnp.dot(
        left, right, precision=lax.Precision.HIGH, preferred_element_type=jnp.float32
    )


def ancestry(parent):
    linked = {}
    for j in range(parent.shape[0]):
        for m in range(j):
            linked_now = parent[j] == m
            for p in range(m + 1, j):
                linked_now = linked_now | (parent[j] == p) & linked[p, m]
            linked[j, m] = linked_now
    return linked


def couplings(couple, parent):
    linked = ancestry(parent)
    return {
        (j, m): couple[j * (j - 1) // 2 + m] * linked[j, m].astype(jnp.float32)
        for j, m in linked
    }


def inverse_coupling(blocks, count, width):
    inverse = {}
    for m in range(count):
        inverse[m, m] = jnp.eye(width, dtype=jnp.float32)
        for j in range(m + 1, count):
            total = blocks[j, m]
            for q in range(m + 1, j):
                total = total + product(inverse[m, q], blocks[j, q])
            inverse[m, j] = -total
    return inverse


def shards(inv_anc, factor_cols, couple, diag_inv, pattern, parent):
    count, rows_here, width = factor_cols.shape
    col_count, row_count = lax.axis_size("col"), lax.axis_size("row")
    total_width = count * width
    local_block = inv_anc.reshape(inv_anc.shape[0] * inv_anc.shape[2], inv_anc.shape[3])
    first_row = (lax.axis_index("row") * col_count + lax.axis_index("col")) * rows_here
    block_ids = (first_row + jnp.arange(rows_here, dtype=jnp.int32)) // width
    row_mask = jnp.take(pattern, block_ids, axis=1).astype(jnp.float32)
    masked = factor_cols * row_mask[:, :, None]
    blocks = couplings(couple, parent)
    reduced = []
    for j in range(count):
        current = masked[j]
        for m in range(j):
            current = current - product(reduced[m], blocks[j, m])
        reduced.append(current)
    joined = jnp.concatenate(reduced, axis=1)
    gathered = lax.all_gather(joined, "col", axis=0, tiled=True)
    partial_value = product(local_block, gathered)
    summed = lax.psum_scatter(partial_value, "row", scatter_dimension=0, tiled=True)
    columns = jnp.stack([-summed[:, j * width : (j + 1) * width] for j in range(count)])
    inverse = inverse_coupling(blocks, count, width)
    zero = jnp.zeros((width, width), jnp.float32)
    whole = jnp.concatenate(
        [
            jnp.concatenate([inverse.get((m, j), zero) for j in range(count)], axis=1)
            for m in range(count)
        ],
        axis=0,
    )
    slab = total_width // col_count
    own = lax.dynamic_slice_in_dim(whole, lax.axis_index("col") * slab, slab, axis=1)
    weighted = jnp.concatenate(
        [product(own[q * width : (q + 1) * width].T, diag_inv[q]) for q in range(count)],
        axis=1,
    )
    window = product(weighted, whole)
    exchanged = lax.all_to_all(summed, "col", split_axis=1, concat_axis=0, tiled=True)
    slab_rows = lax.psum_scatter(
        product(exchanged.T, gathered), "row", scatter_dimension=0, tiled=True
    )
    part = slab // row_count
    slab_rows = slab_rows + lax.dynamic_slice_in_dim(
        window, lax.axis_index("row") * part, part, axis=0
    )
    full = lax.all_gather(slab_rows, ("col", "row"), axis=0, tiled=True)

    def block(m, j):
        return full[m * width : (m + 1) * width, j * width : (j + 1) * width]

    pairs = jnp.stack([block(m, j) for j in range(count) for m in range(j)])
    diagonal = jnp.stack([block(j, j) for j in range(count)])
    return columns, pairs, diagonal


def solution(mesh):
    in_specs = (P(None, "col", None, "row"), P(None, ("row", "col"), None), P(), P(), P(), P())
    out_specs = (P(None, ("row", "col"), None), P(), P())
    return jax.shard_map(shards, mesh=mesh, in_specs=in_specs, out_specs=out_specs, check_vma=False)
```

```python
import functools

import jax
import jax.numpy as jnp
from jax import lax
from jax.experimental import pallas as pl
from jax.experimental.pallas import tpu as pltpu
from jax.sharding import PartitionSpec as P

MESH = pl.DeviceIdType.MESH


def product(left, right):
    return jnp.dot(
        left, right, precision=lax.Precision.HIGH, preferred_element_type=jnp.float32
    )


def ancestry(parent):
    linked = {}
    for j in range(parent.shape[0]):
        for m in range(j):
            linked_now = parent[j] == m
            for p in range(m + 1, j):
                linked_now = linked_now | (parent[j] == p) & linked[p, m]
            linked[j, m] = linked_now
    return linked


def couplings(couple, parent):
    linked = ancestry(parent)
    return {
        (j, m): couple[j * (j - 1) // 2 + m] * linked[j, m].astype(jnp.float32)
        for j, m in linked
    }


def inverse_coupling(blocks, count, width):
    inverse = {}
    for m in range(count):
        inverse[m, m] = jnp.eye(width, dtype=jnp.float32)
        for j in range(m + 1, count):
            total = blocks[j, m]
            for q in range(m + 1, j):
                total = total + product(inverse[m, q], blocks[j, q])
            inverse[m, j] = -total
    return inverse


def shards(inv_anc, factor_cols, couple, diag_inv, pattern, parent):
    count, rows_here, width = factor_cols.shape
    col_count, row_count = lax.axis_size("col"), lax.axis_size("row")
    total_width = count * width
    local_block = inv_anc.reshape(inv_anc.shape[0] * inv_anc.shape[2], inv_anc.shape[3])
    first_row = (lax.axis_index("row") * col_count + lax.axis_index("col")) * rows_here
    block_ids = (first_row + jnp.arange(rows_here, dtype=jnp.int32)) // width
    row_mask = jnp.take(pattern, block_ids, axis=1).astype(jnp.float32)
    masked = factor_cols * row_mask[:, :, None]
    blocks = couplings(couple, parent)
    reduced = []
    for j in range(count):
        current = masked[j]
        for m in range(j):
            current = current - product(reduced[m], blocks[j, m])
        reduced.append(current)
    joined = jnp.concatenate(reduced, axis=1)
    gathered = lax.all_gather(joined, "col", axis=0, tiled=True)
    partial_value = product(local_block, gathered)
    summed = lax.psum_scatter(partial_value, "row", scatter_dimension=0, tiled=True)
    columns = jnp.stack([-summed[:, j * width : (j + 1) * width] for j in range(count)])
    inverse = inverse_coupling(blocks, count, width)
    zero = jnp.zeros((width, width), jnp.float32)
    whole = jnp.concatenate(
        [
            jnp.concatenate([inverse.get((m, j), zero) for j in range(count)], axis=1)
            for m in range(count)
        ],
        axis=0,
    )
    slab = total_width // col_count
    own = lax.dynamic_slice_in_dim(whole, lax.axis_index("col") * slab, slab, axis=1)
    weighted = jnp.concatenate(
        [product(own[q * width : (q + 1) * width].T, diag_inv[q]) for q in range(count)],
        axis=1,
    )
    window = product(weighted, whole)
    exchanged = lax.all_to_all(summed, "col", split_axis=1, concat_axis=0, tiled=True)
    slab_rows = lax.psum_scatter(
        product(exchanged.T, gathered), "row", scatter_dimension=0, tiled=True
    )
    part = slab // row_count
    slab_rows = slab_rows + lax.dynamic_slice_in_dim(
        window, lax.axis_index("row") * part, part, axis=0
    )
    full = lax.all_gather(slab_rows, ("col", "row"), axis=0, tiled=True)

    def block(m, j):
        return full[m * width : (m + 1) * width, j * width : (j + 1) * width]

    pairs = jnp.stack([block(m, j) for j in range(count) for m in range(j)])
    diagonal = jnp.stack([block(j, j) for j in range(count)])
    return columns, pairs, diagonal


def split(value):
    high = value.astype(jnp.bfloat16)
    return high, (value - high.astype(jnp.float32)).astype(jnp.bfloat16)


def dot3(left, right):
    (a, b), (c, d) = left, right
    return (
        jnp.dot(a, c, preferred_element_type=jnp.float32)
        + jnp.dot(a, d, preferred_element_type=jnp.float32)
        + jnp.dot(b, c, preferred_element_type=jnp.float32)
    )


def window_kernel(
    n_col, pattern, parent, anc, factor, couple, diag, cols_out, win_out,
    links, inverse, gath, ypart, xbuf, yown, ysl, gpart, gbuf,
    z_s, z_r, y_s, y_r, k_s, k_r, x_s, x_r, a_s, a_r, b_s, b_r, g_s, g_r,
    fz_s, fz_r, fp_s, fp_r, fq_s, fq_r, fk_s, fk_r,
):
    count, rows, width = factor.shape
    n_z, n_chip, slab = n_col // 4, n_col // 2, ysl.shape[1]
    halves = width // slab
    npair = couple.shape[0]
    r, c = lax.axis_index("row"), lax.axis_index("col")
    core, chip = c % 2, c // 2
    y, z = chip % 2, chip // 2

    def col_of(zz, yy, kk):
        return (zz * 2 + yy) * 2 + kk

    def behind(d):
        return (z + n_z - d) % n_z

    barrier = pltpu.get_barrier_semaphore()
    for e in range(1, n_col):
        pl.semaphore_signal(barrier, inc=1, device_id=(r, (c + e) % n_col), device_id_type=MESH)
    pl.semaphore_signal(barrier, inc=1, device_id=(1 - r, c), device_id_type=MESH)

    def remote(src, dst, send, recv, device):
        return pltpu.make_async_remote_copy(
            src_ref=src, dst_ref=dst, send_sem=send, recv_sem=recv,
            device_id=device, device_id_type=MESH,
        )

    y_dev, k_dev, x_dev = (r, col_of(z, 1 - y, core)), (r, col_of(z, y, 1 - core)), (1 - r, c)
    ended = []

    def begin(copy):
        copy.start()
        ended.append(copy)

    def slot(j, index):
        return gath.at[j, pl.ds(pl.multiple_of(index * rows, 16), rows), :]

    linked = {}
    for j in range(count):
        for m in range(j):
            now = parent[j] == m
            for p in range(m + 1, j):
                now = jnp.logical_or(now, jnp.logical_and(parent[j] == p, linked[p, m]))
            linked[j, m] = now
            pair = j * (j - 1) // 2 + m
            links[pair] = couple[pair] * jnp.where(now, 1.0, 0.0)
    first_row = (r * n_col + c) * rows
    first_block, last_block = first_row // width, (first_row + rows - 1) // width
    inside = lax.broadcasted_iota(jnp.int32, (rows, width), 0) < (first_block + 1) * width - first_row

    reduced = []
    for j in range(count):
        mask = jnp.where(
            inside,
            pattern[j, first_block].astype(jnp.float32),
            pattern[j, last_block].astype(jnp.float32),
        )
        current = factor[j] * mask
        for m in range(j):
            current = current - dot3(reduced[m], split(links[j * (j - 1) // 2 + m]))
        reduced.append(split(current))
        gath[j, pl.ds(pl.multiple_of(c * rows, 16), rows), :] = current
        if j == 0:
            pl.semaphore_wait(barrier, n_col)
        own = slot(j, c)
        begin(remote(own, own, y_s.at[j, 0], y_r.at[j, 0], y_dev))
        for d in range(1, n_z):
            there = (r, col_of((z + d) % n_z, y, core))
            begin(remote(own, own, z_s.at[j, d], z_r.at[j, d], there))
        begin(remote(own, own, k_s.at[j, 0], k_r.at[j, 0], k_dev))

    diagonal = (
        lax.broadcasted_iota(jnp.int32, (width, width), 0)
        == lax.broadcasted_iota(jnp.int32, (width, width), 1)
    )
    for m in range(count):
        inverse[m, m] = jnp.where(diagonal, 1.0, 0.0)
        for j in range(m):
            inverse[m, j] = jnp.zeros((width, width), jnp.float32)
        for j in range(m + 1, count):
            total = links[j * (j - 1) // 2 + m]
            for q in range(m + 1, j):
                total = total + dot3(split(inverse[m, q]), split(links[j * (j - 1) // 2 + q]))
            inverse[m, j] = -total

    for j in range(count):
        for d in range(1, n_z):
            piece = slot(j, col_of(behind(d), y, core))
            remote(piece, piece, z_s.at[j, d], z_r.at[j, d], y_dev).wait_recv()
            begin(remote(piece, piece, y_s.at[j, d], y_r.at[j, d], y_dev))
            begin(remote(piece, piece, k_s.at[j, d], k_r.at[j, d], k_dev))

    m, h = chip // halves, chip % halves

    def q_of(rr):
        rho = (rr + z) % 2
        return (1 - core) * 3 * rho + core * (2 - rho)

    q_own, q_other = q_of(r), q_of(1 - r)
    j_own, j_other = jnp.minimum(m + q_own, count - 1), jnp.minimum(m + q_other, count - 1)
    half = pl.ds(pl.multiple_of(h * slab, slab), slab)
    piece_sum = jnp.zeros((slab, width), jnp.float32)
    for q in range(count):
        left = inverse[q, m, :, half].T
        middle = dot3(split(left), split(diag[q]))
        piece_sum = piece_sum + dot3(split(middle), split(inverse[q, j_own]))
    gpart[2] = piece_sum

    left_anc = split(anc[...].reshape(2 * rows, anc.shape[2]))

    def relay(j):
        for d in range(n_z):
            piece = slot(j, col_of(behind(d), 1 - y, core))
            remote(piece, piece, y_s.at[j, d], y_r.at[j, d], y_dev).wait_recv()
            begin(remote(piece, piece, k_s.at[j, n_z + d], k_r.at[j, n_z + d], k_dev))

    def multiply(j):
        for d in range(n_z):
            for side, yy in ((0, y), (1, 1 - y)):
                piece = slot(j, col_of(behind(d), yy, 1 - core))
                at = side * n_z + d
                remote(piece, piece, k_s.at[j, at], k_r.at[j, at], k_dev).wait_recv()
        ypart[j] = dot3(left_anc, split(gath[j])).reshape(2, rows, width)
        begin(remote(ypart.at[j, 1 - r], xbuf.at[j], x_s.at[j], x_r.at[j], x_dev))

    def scatter(j):
        remote(ypart.at[j, 1 - r], xbuf.at[j], x_s.at[j], x_r.at[j], x_dev).wait_recv()
        total = ypart[j, r] + xbuf[j]
        yown[j] = total
        cols_out[j] = -total
        for part in range(halves):
            s = j * halves + part
            src = yown.at[j, :, pl.ds(part * slab, slab)]
            dst = ysl.at[pl.ds(pl.multiple_of(c * rows, 16), rows), :]

            @pl.when(chip == s)
            def _():
                ysl[pl.ds(pl.multiple_of(c * rows, 16), rows), :] = total[:, part * slab : (part + 1) * slab]

            @pl.when(chip != s)
            def _():
                remote(src, dst, a_s.at[s], a_r.at[chip], (r, 2 * s + core)).start()

    for j in range(count):
        relay(j)
        if j > 0:
            multiply(j - 1)
        if j > 1:
            scatter(j - 2)
    multiply(count - 1)
    scatter(count - 2)
    scatter(count - 1)

    def slab_rows(index):
        return ysl.at[pl.ds(pl.multiple_of(index * rows, 16), rows), :]

    for e in range(n_chip):
        other = (chip + n_chip - e) % n_chip
        piece = slab_rows(2 * other + core)
        if e:
            remote(piece, piece, a_s.at[0], a_r.at[other], k_dev).wait_recv()
        begin(remote(piece, piece, b_s.at[e], b_r.at[e], k_dev))
    for e in range(n_chip):
        other = (chip + n_chip - e) % n_chip
        piece = slab_rows(2 * other + 1 - core)
        remote(piece, piece, b_s.at[e], b_r.at[e], k_dev).wait_recv()
    left = split(ysl[...].T)
    gpart[1] = dot3(left, split(gath[j_other]))
    begin(remote(gpart.at[1], gbuf, g_s, g_r, x_dev))
    gpart[0] = dot3(left, split(gath[j_own])) + gpart[2]
    remote(gpart.at[1], gbuf, g_s, g_r, x_dev).wait_recv()

    def place(rr, zz, yy, kk):
        rho = (rr + zz) % 2
        q = (1 - kk) * 3 * rho + kk * (2 - rho)
        block, part = (2 * zz + yy) // halves, (2 * zz + yy) % halves
        j = block + q
        off = (q + 3) // 4
        index = off * (j * (j - 1) // 2 + block) + (1 - off) * (npair + block)
        return j < count, index * 1, part

    def at_piece(where):
        _, index, part = where
        return win_out.at[index, pl.ds(pl.multiple_of(part * slab, slab), slab), :]

    flip_y, flip_x = 1 - 2 * y, 1 - 2 * r
    r1, y1 = r + core * flip_x, y + (1 - core) * flip_y
    r2, y2 = r + (1 - core) * flip_x, y + core * flip_y
    p_dev, q_dev = (r1, col_of(z, y1, core)), (r2, col_of(z, y2, core))
    late = []

    def later(needed, copy):
        @pl.when(needed)
        def _():
            copy().start()

        late.append((needed, copy))

    def send(where, send_sem, recv_sem, device):
        def copy():
            piece = at_piece(where)
            return remote(piece, piece, send_sem, recv_sem, device)

        later(where[0], copy)

    def receive(where, send_sem, recv_sem, device):
        @pl.when(where[0])
        def _():
            piece = at_piece(where)
            remote(piece, piece, send_sem, recv_sem, device).wait_recv()

    mine = place(r, z, y, core)

    @pl.when(mine[0])
    def _():
        win_out[mine[1], pl.ds(pl.multiple_of(mine[2] * slab, slab), slab), :] = gpart[0] + gbuf[...]

    for d in range(1, n_z):
        send(mine, fz_s.at[d], fz_r.at[d], (r, col_of((z + d) % n_z, y, core)))
    for d in range(n_z):
        where = place(r, behind(d), y, core)
        if d:
            receive(where, fz_s.at[d], fz_r.at[d], k_dev)
        send(where, fp_s.at[d], fp_r.at[d], p_dev)
        send(where, fq_s.at[d], fq_r.at[d], q_dev)
        send(where, fk_s.at[d], fk_r.at[d], k_dev)
    for d in range(n_z):
        where = place(r1, behind(d), y1, core)
        receive(where, fp_s.at[d], fp_r.at[d], k_dev)
        send(where, fq_s.at[n_z + d], fq_r.at[n_z + d], q_dev)
        send(where, fk_s.at[n_z + d], fk_r.at[n_z + d], k_dev)
    for side, (rr, yy) in enumerate(((r2, y2), (1 - r, 1 - y))):
        for d in range(n_z):
            where, at = place(rr, behind(d), yy, core), side * n_z + d
            receive(where, fq_s.at[at], fq_r.at[at], k_dev)
            send(where, fk_s.at[2 * n_z + at], fk_r.at[2 * n_z + at], k_dev)
    for side, (rr, yy) in enumerate(((r, y), (r2, y2), (r1, y1), (1 - r, 1 - y))):
        for d in range(n_z):
            where, at = place(rr, behind(d), yy, 1 - core), side * n_z + d
            receive(where, fk_s.at[at], fk_r.at[at], k_dev)

    for copy in ended:
        copy.wait_send()
    for s in range(n_chip):
        @pl.when(chip != s)
        def _():
            src = yown.at[s // halves, :, pl.ds((s % halves) * slab, slab)]
            remote(src, slab_rows(c), a_s.at[s], a_r.at[chip], (r, 2 * s + core)).wait_send()
    for needed, copy in late:
        @pl.when(needed)
        def _():
            copy().wait_send()


def one_kernel(inv_anc, factor_cols, couple, diag_inv, pattern, parent):
    n_col = lax.axis_size("col")
    count, rows, width = factor_cols.shape
    npair = couple.shape[0]
    n_z, n_chip = n_col // 4, n_col // 2
    slab = count * width // n_chip
    vmem, smem = pl.BlockSpec(memory_space=pltpu.VMEM), pl.BlockSpec(memory_space=pltpu.SMEM)
    buffer = lambda *shape: pltpu.VMEM(shape, jnp.float32)
    sems = lambda *shape: pltpu.SemaphoreType.DMA(shape)
    twice = lambda *shape: [sems(*shape), sems(*shape)]
    columns, window = pl.pallas_call(
        functools.partial(window_kernel, n_col),
        out_shape=(
            jax.ShapeDtypeStruct((count, rows, width), jnp.float32),
            jax.ShapeDtypeStruct((npair + count, width, width), jnp.float32),
        ),
        in_specs=[smem, smem, vmem, vmem, vmem, vmem],
        out_specs=(vmem, vmem),
        scratch_shapes=[
            buffer(npair, width, width),
            buffer(count, count, width, width),
            buffer(count, n_col * rows, width),
            buffer(count, 2, rows, width),
            buffer(count, rows, width),
            buffer(count, rows, width),
            buffer(n_col * rows, slab),
            buffer(3, slab, width),
            buffer(slab, width),
            *twice(count, n_z),
            *twice(count, n_z),
            *twice(count, 2 * n_z),
            *twice(count),
            *twice(n_chip),
            *twice(n_chip),
            pltpu.SemaphoreType.DMA,
            pltpu.SemaphoreType.DMA,
            *twice(n_z),
            *twice(n_z),
            *twice(2 * n_z),
            *twice(4 * n_z),
        ],
        compiler_params=pltpu.CompilerParams(
            collective_id=0, has_side_effects=True, vmem_limit_bytes=48 << 20
        ),
    )(pattern, parent, inv_anc.reshape(-1, rows, inv_anc.shape[3]), factor_cols, couple, diag_inv)
    return columns, window[:npair], window[npair:]


def solution(mesh):
    in_specs = (P(None, "col", None, "row"), P(None, ("row", "col"), None), P(), P(), P(), P())
    out_specs = (P(None, ("row", "col"), None), P(), P())

    def body(inv_anc, factor_cols, couple, diag_inv, pattern, parent):
        count, rows, width = factor_cols.shape
        slab = count * width // (mesh.shape["col"] // 2)
        fits = mesh.shape["row"] == 2 and mesh.shape["col"] == 4 * count
        fits = fits and slab % 128 == 0 and rows % 16 == 0 and rows <= width and count == 4
        run = one_kernel if fits else shards
        return run(inv_anc, factor_cols, couple, diag_inv, pattern, parent)

    return jax.shard_map(body, mesh=mesh, in_specs=in_specs, out_specs=out_specs, check_vma=False)
```

```python
import functools

import jax
import jax.numpy as jnp
from jax import lax
from jax.experimental import pallas as pl
from jax.experimental.pallas import tpu as pltpu
from jax.sharding import PartitionSpec as P

MESH = pl.DeviceIdType.MESH


def product(left, right):
    return jnp.dot(
        left, right, precision=lax.Precision.HIGH, preferred_element_type=jnp.float32
    )


def ancestry(parent):
    linked = {}
    for j in range(parent.shape[0]):
        for m in range(j):
            linked_now = parent[j] == m
            for p in range(m + 1, j):
                linked_now = linked_now | (parent[j] == p) & linked[p, m]
            linked[j, m] = linked_now
    return linked


def couplings(couple, parent):
    linked = ancestry(parent)
    return {
        (j, m): couple[j * (j - 1) // 2 + m] * linked[j, m].astype(jnp.float32)
        for j, m in linked
    }


def inverse_coupling(blocks, count, width):
    inverse = {}
    for m in range(count):
        inverse[m, m] = jnp.eye(width, dtype=jnp.float32)
        for j in range(m + 1, count):
            total = blocks[j, m]
            for q in range(m + 1, j):
                total = total + product(inverse[m, q], blocks[j, q])
            inverse[m, j] = -total
    return inverse


def shards(inv_anc, factor_cols, couple, diag_inv, pattern, parent):
    count, rows_here, width = factor_cols.shape
    col_count, row_count = lax.axis_size("col"), lax.axis_size("row")
    total_width = count * width
    local_block = inv_anc.reshape(inv_anc.shape[0] * inv_anc.shape[2], inv_anc.shape[3])
    first_row = (lax.axis_index("row") * col_count + lax.axis_index("col")) * rows_here
    block_ids = (first_row + jnp.arange(rows_here, dtype=jnp.int32)) // width
    row_mask = jnp.take(pattern, block_ids, axis=1).astype(jnp.float32)
    masked = factor_cols * row_mask[:, :, None]
    blocks = couplings(couple, parent)
    reduced = []
    for j in range(count):
        current = masked[j]
        for m in range(j):
            current = current - product(reduced[m], blocks[j, m])
        reduced.append(current)
    joined = jnp.concatenate(reduced, axis=1)
    gathered = lax.all_gather(joined, "col", axis=0, tiled=True)
    partial_value = product(local_block, gathered)
    summed = lax.psum_scatter(partial_value, "row", scatter_dimension=0, tiled=True)
    columns = jnp.stack([-summed[:, j * width : (j + 1) * width] for j in range(count)])
    inverse = inverse_coupling(blocks, count, width)
    zero = jnp.zeros((width, width), jnp.float32)
    whole = jnp.concatenate(
        [
            jnp.concatenate([inverse.get((m, j), zero) for j in range(count)], axis=1)
            for m in range(count)
        ],
        axis=0,
    )
    slab = total_width // col_count
    own = lax.dynamic_slice_in_dim(whole, lax.axis_index("col") * slab, slab, axis=1)
    weighted = jnp.concatenate(
        [product(own[q * width : (q + 1) * width].T, diag_inv[q]) for q in range(count)],
        axis=1,
    )
    window = product(weighted, whole)
    exchanged = lax.all_to_all(summed, "col", split_axis=1, concat_axis=0, tiled=True)
    slab_rows = lax.psum_scatter(
        product(exchanged.T, gathered), "row", scatter_dimension=0, tiled=True
    )
    part = slab // row_count
    slab_rows = slab_rows + lax.dynamic_slice_in_dim(
        window, lax.axis_index("row") * part, part, axis=0
    )
    full = lax.all_gather(slab_rows, ("col", "row"), axis=0, tiled=True)

    def block(m, j):
        return full[m * width : (m + 1) * width, j * width : (j + 1) * width]

    pairs = jnp.stack([block(m, j) for j in range(count) for m in range(j)])
    diagonal = jnp.stack([block(j, j) for j in range(count)])
    return columns, pairs, diagonal


def split(value):
    high = value.astype(jnp.bfloat16)
    return high, (value - high.astype(jnp.float32)).astype(jnp.bfloat16)


def dot3(left, right):
    (a, b), (c, d) = left, right
    return (
        jnp.dot(a, c, preferred_element_type=jnp.float32)
        + jnp.dot(a, d, preferred_element_type=jnp.float32)
        + jnp.dot(b, c, preferred_element_type=jnp.float32)
    )


def window_kernel(
    n_col, pattern_in, parent_in, anc_in, factor_in, couple_in, diag_in, cols_out, win_out,
    pattern, parent, anc, factor, couple, diag, in_s, links, inverse, gath, ypart, xbuf, yown, ysl, gpart, gbuf,
    z_s, z_r, y_s, y_r, k_s, k_r, x_s, x_r, a_s, a_r, b_s, b_r, g_s, g_r,
    fz_s, fz_r, fp_s, fp_r, fq_s, fq_r, fk_s, fk_r,
):
    count, rows, width = factor.shape
    n_z, n_chip, slab = n_col // 4, n_col // 2, ysl.shape[1]
    halves = width // slab
    npair = couple.shape[0]
    r, c = lax.axis_index("row"), lax.axis_index("col")
    core, chip = c % 2, c // 2
    y, z = chip % 2, chip // 2

    def col_of(zz, yy, kk):
        return (zz * 2 + yy) * 2 + kk

    def behind(d):
        return (z + n_z - d) % n_z

    def slab_of(cc):
        return (cc + n_chip - 2) % n_chip

    mine_slab = slab_of(chip)

    loads = [
        pltpu.make_async_copy(src, dst, in_s.at[i])
        for i, (src, dst) in enumerate(
            (
                (factor_in, factor), (pattern_in, pattern), (parent_in, parent),
                (couple_in, couple), (diag_in, diag), (anc_in, anc),
            )
        )
    ]
    for load in loads:
        load.start()
    barrier = pltpu.get_barrier_semaphore()
    for e in range(1, n_col):
        pl.semaphore_signal(barrier, inc=1, device_id=(r, (c + e) % n_col), device_id_type=MESH)
    pl.semaphore_signal(barrier, inc=1, device_id=(1 - r, c), device_id_type=MESH)

    def remote(src, dst, send, recv, device):
        return pltpu.make_async_remote_copy(
            src_ref=src, dst_ref=dst, send_sem=send, recv_sem=recv,
            device_id=device, device_id_type=MESH,
        )

    y_dev, k_dev, x_dev = (r, col_of(z, 1 - y, core)), (r, col_of(z, y, 1 - core)), (1 - r, c)
    late = []

    def begin(copy):
        copy.start()
        late.append((None, lambda: copy))

    def later(needed, copy):
        @pl.when(needed)
        def _():
            copy().start()

        late.append((needed, copy))

    def slot(j, index):
        return gath.at[j, pl.ds(pl.multiple_of(index * rows, 16), rows), :]

    first_row = (r * n_col + c) * rows
    first_block, last_block = first_row // width, (first_row + rows - 1) // width
    inside = lax.broadcasted_iota(jnp.int32, (rows, width), 0) < (first_block + 1) * width - first_row

    def along(j, step, d, index):
        to = z - step
        piece = lambda: slot(j, index)
        side = (step + 1) // 2

        def copy():
            there = (r, col_of((to + n_z) % n_z, y, core))
            return remote(piece(), piece(), z_s.at[j, side, d], z_r.at[j, side, d], there)

        return jnp.logical_and(to >= 0, to < n_z), copy

    reduced, coupled = [], {}
    loads[0].wait()
    loads[1].wait()
    for j in range(count):
        mask = jnp.where(
            inside,
            pattern[j, first_block].astype(jnp.float32),
            pattern[j, last_block].astype(jnp.float32),
        )
        current = factor[j] * mask
        for m in range(j):
            current = current - dot3(reduced[m], coupled[j, m])
        reduced.append(split(current))
        gath[j, pl.ds(pl.multiple_of(c * rows, 16), rows), :] = current
        if j == 0:
            pl.semaphore_wait(barrier, n_col)
        own = slot(j, c)
        begin(remote(own, own, y_s.at[j, z], y_r.at[j, z], y_dev))
        for step in (-1, 1):
            later(*along(j, step, 1, c))
        begin(remote(own, own, k_s.at[j, y * n_z + z], k_r.at[j, y * n_z + z], k_dev))
        if j == 0:
            loads[2].wait()
            loads[3].wait()
            linked = {}
        if j + 1 < count:
            for m in range(j + 1):
                now = parent[j + 1] == m
                for p in range(m + 1, j + 1):
                    now = jnp.logical_or(now, jnp.logical_and(parent[j + 1] == p, linked[p, m]))
                linked[j + 1, m] = now
                pair = (j + 1) * j // 2 + m
                links[pair] = couple[pair] * jnp.where(now, 1.0, 0.0)
                coupled[j + 1, m] = split(links[pair])

    diagonal = (
        lax.broadcasted_iota(jnp.int32, (width, width), 0)
        == lax.broadcasted_iota(jnp.int32, (width, width), 1)
    )
    for m in range(count):
        inverse[m, m] = jnp.where(diagonal, 1.0, 0.0)
        for j in range(m):
            inverse[m, j] = jnp.zeros((width, width), jnp.float32)
        for j in range(m + 1, count):
            total = links[j * (j - 1) // 2 + m]
            for q in range(m + 1, j):
                total = total + dot3(split(inverse[m, q]), coupled[j, q])
            inverse[m, j] = -total

    for d in range(1, n_z):
        for j in range(count):
            for step in (-1, 1):
                source = z + step * d
                from_z = (source + n_z) % n_z
                index = col_of(from_z, y, core)
                side = (step + 1) // 2
                there = jnp.logical_and(source >= 0, source < n_z)

                def to_y(j=j, index=index, from_z=from_z):
                    piece = slot(j, index)
                    return remote(piece, piece, y_s.at[j, from_z], y_r.at[j, from_z], y_dev)

                def to_core(j=j, index=index, from_z=from_z):
                    piece, at = slot(j, index), y * n_z + from_z
                    return remote(piece, piece, k_s.at[j, at], k_r.at[j, at], k_dev)

                @pl.when(there)
                def _():
                    piece = slot(j, index)
                    remote(piece, piece, z_s.at[j, side, d], z_r.at[j, side, d], k_dev).wait_recv()

                if d + 1 < n_z:
                    further, onward = along(j, step, d + 1, index)
                    later(jnp.logical_and(there, further), onward)
                later(there, to_y)
                later(there, to_core)

    m, h = mine_slab // halves, mine_slab % halves

    def q_of(rr):
        rho = (rr + z) % 2
        return (1 - core) * 3 * rho + core * (2 - rho)

    q_own, q_other = q_of(r), q_of(1 - r)
    j_own, j_other = jnp.minimum(m + q_own, count - 1), jnp.minimum(m + q_other, count - 1)
    half = pl.ds(pl.multiple_of(h * slab, slab), slab)
    piece_sum = jnp.zeros((slab, width), jnp.float32)
    loads[4].wait()
    for q in range(count):
        left = inverse[q, m, :, half].T
        middle = dot3(split(left), split(diag[q]))
        piece_sum = piece_sum + dot3(split(middle), split(inverse[q, j_own]))
    gpart[2] = piece_sum

    loads[5].wait()
    left_anc = split(anc[...].reshape(2 * rows, anc.shape[2]))

    def relay(j):
        for d in range(n_z):
            from_z = behind(d)
            piece, at = slot(j, col_of(from_z, 1 - y, core)), (1 - y) * n_z + from_z
            remote(piece, piece, y_s.at[j, from_z], y_r.at[j, from_z], y_dev).wait_recv()
            begin(remote(piece, piece, k_s.at[j, at], k_r.at[j, at], k_dev))

    def multiply(j):
        for yy in range(2):
            for zz in range(n_z):
                piece, at = slot(j, col_of(zz, yy, 1 - core)), yy * n_z + zz
                remote(piece, piece, k_s.at[j, at], k_r.at[j, at], k_dev).wait_recv()
        ypart[j] = dot3(left_anc, split(gath[j])).reshape(2, rows, width)
        begin(remote(ypart.at[j, 1 - r], xbuf.at[j], x_s.at[j], x_r.at[j], x_dev))

    def scatter(j):
        remote(ypart.at[j, 1 - r], xbuf.at[j], x_s.at[j], x_r.at[j], x_dev).wait_recv()
        total = ypart[j, r] + xbuf[j]
        yown[j] = total
        cols_out[j] = -total
        for part in range(halves):
            s = j * halves + part
            target = (s + 2) % n_chip
            src = yown.at[j, :, pl.ds(part * slab, slab)]
            dst = ysl.at[pl.ds(pl.multiple_of(c * rows, 16), rows), :]

            @pl.when(chip == target)
            def _():
                ysl[pl.ds(pl.multiple_of(c * rows, 16), rows), :] = total[:, part * slab : (part + 1) * slab]

            @pl.when(chip != target)
            def _():
                remote(src, dst, a_s.at[s], a_r.at[chip], (r, 2 * target + core)).start()

    for j in range(count):
        relay(j)
        if j > 0:
            multiply(j - 1)
        if j > 1:
            scatter(j - 2)
    multiply(count - 1)
    scatter(count - 2)
    scatter(count - 1)

    def slab_rows(index):
        return ysl.at[pl.ds(pl.multiple_of(index * rows, 16), rows), :]

    for e in range(n_chip):
        other = (chip + n_chip - e) % n_chip
        piece = slab_rows(2 * other + core)
        if e:
            remote(piece, piece, a_s.at[0], a_r.at[other], k_dev).wait_recv()
        begin(remote(piece, piece, b_s.at[e], b_r.at[e], k_dev))
    for e in range(n_chip):
        other = (chip + n_chip - e) % n_chip
        piece = slab_rows(2 * other + 1 - core)
        remote(piece, piece, b_s.at[e], b_r.at[e], k_dev).wait_recv()
    left = split(ysl[...].T)
    gpart[1] = dot3(left, split(gath[j_other]))
    begin(remote(gpart.at[1], gbuf, g_s, g_r, x_dev))
    gpart[0] = dot3(left, split(gath[j_own])) + gpart[2]
    remote(gpart.at[1], gbuf, g_s, g_r, x_dev).wait_recv()

    def place(rr, zz, yy, kk):
        rho = (rr + zz) % 2
        q = (1 - kk) * 3 * rho + kk * (2 - rho)
        block, part = slab_of(2 * zz + yy) // halves, slab_of(2 * zz + yy) % halves
        j = block + q
        off = (q + 3) // 4
        index = off * (j * (j - 1) // 2 + block) + (1 - off) * (npair + block)
        return j < count, index * 1, part

    def at_piece(where):
        _, index, part = where
        return win_out.at[index, pl.ds(pl.multiple_of(part * slab, slab), slab), :]

    flip_y, flip_x = 1 - 2 * y, 1 - 2 * r
    r1, y1 = r + core * flip_x, y + (1 - core) * flip_y
    r2, y2 = r + (1 - core) * flip_x, y + core * flip_y
    p_dev, q_dev = (r1, col_of(z, y1, core)), (r2, col_of(z, y2, core))
    def send(where, send_sem, recv_sem, device):
        def copy():
            piece = at_piece(where)
            return remote(piece, piece, send_sem, recv_sem, device)

        later(where[0], copy)

    def receive(where, send_sem, recv_sem, device):
        @pl.when(where[0])
        def _():
            piece = at_piece(where)
            remote(piece, piece, send_sem, recv_sem, device).wait_recv()

    mine = place(r, z, y, core)

    @pl.when(mine[0])
    def _():
        win_out[mine[1], pl.ds(pl.multiple_of(mine[2] * slab, slab), slab), :] = gpart[0] + gbuf[...]

    for d in range(1, n_z):
        send(mine, fz_s.at[d], fz_r.at[d], (r, col_of((z + d) % n_z, y, core)))
    for d in range(n_z):
        where = place(r, behind(d), y, core)
        if d:
            receive(where, fz_s.at[d], fz_r.at[d], k_dev)
        send(where, fp_s.at[d], fp_r.at[d], p_dev)
        send(where, fq_s.at[d], fq_r.at[d], q_dev)
        send(where, fk_s.at[d], fk_r.at[d], k_dev)
    for d in range(n_z):
        where = place(r1, behind(d), y1, core)
        receive(where, fp_s.at[d], fp_r.at[d], k_dev)
        send(where, fq_s.at[n_z + d], fq_r.at[n_z + d], q_dev)
        send(where, fk_s.at[n_z + d], fk_r.at[n_z + d], k_dev)
    for side, (rr, yy) in enumerate(((r2, y2), (1 - r, 1 - y))):
        for d in range(n_z):
            where, at = place(rr, behind(d), yy, core), side * n_z + d
            receive(where, fq_s.at[at], fq_r.at[at], k_dev)
            send(where, fk_s.at[2 * n_z + at], fk_r.at[2 * n_z + at], k_dev)
    for side, (rr, yy) in enumerate(((r, y), (r2, y2), (r1, y1), (1 - r, 1 - y))):
        for d in range(n_z):
            where, at = place(rr, behind(d), yy, 1 - core), side * n_z + d
            receive(where, fk_s.at[at], fk_r.at[at], k_dev)

    for s in range(n_chip):
        target = (s + 2) % n_chip

        @pl.when(chip != target)
        def _():
            src = yown.at[s // halves, :, pl.ds((s % halves) * slab, slab)]
            remote(src, slab_rows(c), a_s.at[s], a_r.at[chip], (r, 2 * target + core)).wait_send()
    for needed, copy in late:
        if needed is None:
            copy().wait_send()
        else:
            @pl.when(needed)
            def _():
                copy().wait_send()


def deliver(npair, columns, window, cols_out, pairs_out, diag_out, done):
    parts = ((window.at[:npair], pairs_out), (window.at[npair:], diag_out), (columns, cols_out))
    copies = [pltpu.make_async_copy(src, dst, done.at[i]) for i, (src, dst) in enumerate(parts)]
    for copy in copies:
        copy.start()
    for copy in copies:
        copy.wait()


def one_kernel(inv_anc, factor_cols, couple, diag_inv, pattern, parent):
    n_col = lax.axis_size("col")
    count, rows, width = factor_cols.shape
    npair = couple.shape[0]
    n_z, n_chip = n_col // 4, n_col // 2
    slab = count * width // n_chip
    vmem, hbm = pl.BlockSpec(memory_space=pltpu.VMEM), pl.BlockSpec(memory_space=pltpu.HBM)
    anywhere = pl.BlockSpec(memory_space=pl.ANY)
    anc = inv_anc.reshape(-1, rows, inv_anc.shape[3])
    buffer = lambda *shape: pltpu.VMEM(shape, jnp.float32)
    sems = lambda *shape: pltpu.SemaphoreType.DMA(shape)
    twice = lambda *shape: [sems(*shape), sems(*shape)]
    columns, window = pl.pallas_call(
        functools.partial(window_kernel, n_col),
        out_shape=(
            jax.ShapeDtypeStruct((count, rows, width), jnp.float32),
            jax.ShapeDtypeStruct((npair + count, width, width), jnp.float32),
        ),
        in_specs=[hbm] * 6,
        out_specs=(vmem, vmem),
        scratch_shapes=[
            pltpu.SMEM(pattern.shape, jnp.int32),
            pltpu.SMEM(parent.shape, jnp.int32),
            buffer(*anc.shape),
            buffer(*factor_cols.shape),
            buffer(*couple.shape),
            buffer(*diag_inv.shape),
            sems(6),
            buffer(npair, width, width),
            buffer(count, count, width, width),
            buffer(count, n_col * rows, width),
            buffer(count, 2, rows, width),
            buffer(count, rows, width),
            buffer(count, rows, width),
            buffer(n_col * rows, slab),
            buffer(3, slab, width),
            buffer(slab, width),
            *twice(count, 2, n_z),
            *twice(count, n_z),
            *twice(count, 2 * n_z),
            *twice(count),
            *twice(n_chip),
            *twice(n_chip),
            pltpu.SemaphoreType.DMA,
            pltpu.SemaphoreType.DMA,
            *twice(n_z),
            *twice(n_z),
            *twice(2 * n_z),
            *twice(4 * n_z),
        ],
        compiler_params=pltpu.CompilerParams(
            collective_id=0, has_side_effects=True, vmem_limit_bytes=63 << 20
        ),
    )(pattern, parent, anc, factor_cols, couple, diag_inv)
    return pl.pallas_call(
        functools.partial(deliver, npair),
        out_shape=tuple(
            jax.ShapeDtypeStruct(like.shape, jnp.float32) for like in (factor_cols, couple, diag_inv)
        ),
        in_specs=[anywhere] * 2,
        out_specs=(anywhere,) * 3,
        scratch_shapes=[sems(3)],
        compiler_params=pltpu.CompilerParams(vmem_limit_bytes=63 << 20),
    )(columns, window)


def solution(mesh):
    in_specs = (P(None, "col", None, "row"), P(None, ("row", "col"), None), P(), P(), P(), P())
    out_specs = (P(None, ("row", "col"), None), P(), P())

    def body(inv_anc, factor_cols, couple, diag_inv, pattern, parent):
        count, rows, width = factor_cols.shape
        slab = count * width // (mesh.shape["col"] // 2)
        fits = mesh.shape["row"] == 2 and mesh.shape["col"] == 4 * count
        fits = fits and slab % 128 == 0 and rows % 16 == 0 and rows <= width and count == 4
        run = one_kernel if fits else shards
        return run(inv_anc, factor_cols, couple, diag_inv, pattern, parent)

    return jax.shard_map(body, mesh=mesh, in_specs=in_specs, out_specs=out_specs, check_vma=False)
```

```python
import functools

import jax
import jax.numpy as jnp
from jax import lax
from jax.experimental import pallas as pl
from jax.experimental.pallas import tpu as pltpu
from jax.sharding import PartitionSpec as P

MESH = pl.DeviceIdType.MESH


def product(left, right):
    return jnp.dot(
        left, right, precision=lax.Precision.HIGH, preferred_element_type=jnp.float32
    )


def ancestry(parent):
    linked = {}
    for j in range(parent.shape[0]):
        for m in range(j):
            linked_now = parent[j] == m
            for p in range(m + 1, j):
                linked_now = linked_now | (parent[j] == p) & linked[p, m]
            linked[j, m] = linked_now
    return linked


def couplings(couple, parent):
    linked = ancestry(parent)
    return {
        (j, m): couple[j * (j - 1) // 2 + m] * linked[j, m].astype(jnp.float32)
        for j, m in linked
    }


def inverse_coupling(blocks, count, width):
    inverse = {}
    for m in range(count):
        inverse[m, m] = jnp.eye(width, dtype=jnp.float32)
        for j in range(m + 1, count):
            total = blocks[j, m]
            for q in range(m + 1, j):
                total = total + product(inverse[m, q], blocks[j, q])
            inverse[m, j] = -total
    return inverse


def shards(inv_anc, factor_cols, couple, diag_inv, pattern, parent):
    count, rows_here, width = factor_cols.shape
    col_count, row_count = lax.axis_size("col"), lax.axis_size("row")
    total_width = count * width
    local_block = inv_anc.reshape(inv_anc.shape[0] * inv_anc.shape[2], inv_anc.shape[3])
    first_row = (lax.axis_index("row") * col_count + lax.axis_index("col")) * rows_here
    block_ids = (first_row + jnp.arange(rows_here, dtype=jnp.int32)) // width
    row_mask = jnp.take(pattern, block_ids, axis=1).astype(jnp.float32)
    masked = factor_cols * row_mask[:, :, None]
    blocks = couplings(couple, parent)
    reduced = []
    for j in range(count):
        current = masked[j]
        for m in range(j):
            current = current - product(reduced[m], blocks[j, m])
        reduced.append(current)
    joined = jnp.concatenate(reduced, axis=1)
    gathered = lax.all_gather(joined, "col", axis=0, tiled=True)
    partial_value = product(local_block, gathered)
    summed = lax.psum_scatter(partial_value, "row", scatter_dimension=0, tiled=True)
    columns = jnp.stack([-summed[:, j * width : (j + 1) * width] for j in range(count)])
    inverse = inverse_coupling(blocks, count, width)
    zero = jnp.zeros((width, width), jnp.float32)
    whole = jnp.concatenate(
        [
            jnp.concatenate([inverse.get((m, j), zero) for j in range(count)], axis=1)
            for m in range(count)
        ],
        axis=0,
    )
    slab = total_width // col_count
    own = lax.dynamic_slice_in_dim(whole, lax.axis_index("col") * slab, slab, axis=1)
    weighted = jnp.concatenate(
        [product(own[q * width : (q + 1) * width].T, diag_inv[q]) for q in range(count)],
        axis=1,
    )
    window = product(weighted, whole)
    exchanged = lax.all_to_all(summed, "col", split_axis=1, concat_axis=0, tiled=True)
    slab_rows = lax.psum_scatter(
        product(exchanged.T, gathered), "row", scatter_dimension=0, tiled=True
    )
    part = slab // row_count
    slab_rows = slab_rows + lax.dynamic_slice_in_dim(
        window, lax.axis_index("row") * part, part, axis=0
    )
    full = lax.all_gather(slab_rows, ("col", "row"), axis=0, tiled=True)

    def block(m, j):
        return full[m * width : (m + 1) * width, j * width : (j + 1) * width]

    pairs = jnp.stack([block(m, j) for j in range(count) for m in range(j)])
    diagonal = jnp.stack([block(j, j) for j in range(count)])
    return columns, pairs, diagonal


def split(value):
    high = value.astype(jnp.bfloat16)
    return high, (value - high.astype(jnp.float32)).astype(jnp.bfloat16)


def dot3(left, right):
    (a, b), (c, d) = left, right
    return (
        jnp.dot(a, c, preferred_element_type=jnp.float32)
        + jnp.dot(a, d, preferred_element_type=jnp.float32)
        + jnp.dot(b, c, preferred_element_type=jnp.float32)
    )


def window_kernel(
    n_col, pattern_in, parent_in, anc_in, factor_in, couple_in, diag_in, cols_out, win_out,
    pattern, parent, anc, factor, couple, diag, in_s, links, inverse, gath, ypart, xbuf, yown, ysl, gpart, gbuf,
    z_s, z_r, y_s, y_r, k_s, k_r, x_s, x_r, a_s, a_r, b_s, b_r, g_s, g_r,
    fz_s, fz_r, fp_s, fp_r, fq_s, fq_r, fk_s, fk_r,
):
    count, rows, width = factor.shape
    n_z, n_chip, slab = n_col // 4, n_col // 2, ysl.shape[1]
    halves = width // slab
    npair = couple.shape[0]
    r, c = lax.axis_index("row"), lax.axis_index("col")
    core, chip = c % 2, c // 2
    y, z = chip % 2, chip // 2

    def col_of(zz, yy, kk):
        return (zz * 2 + yy) * 2 + kk

    def behind(d):
        return (z + n_z - d) % n_z

    def slab_of(cc):
        return (cc + n_chip - 2) % n_chip

    mine_slab = slab_of(chip)

    loads = [
        pltpu.make_async_copy(src, dst, in_s.at[i])
        for i, (src, dst) in enumerate(
            (
                (factor_in, factor), (pattern_in, pattern), (parent_in, parent),
                (couple_in, couple), (diag_in, diag), (anc_in, anc),
            )
        )
    ]
    for load in loads:
        load.start()
    barrier = pltpu.get_barrier_semaphore()
    for e in range(1, n_col):
        pl.semaphore_signal(barrier, inc=1, device_id=(r, (c + e) % n_col), device_id_type=MESH)
    pl.semaphore_signal(barrier, inc=1, device_id=(1 - r, c), device_id_type=MESH)

    def remote(src, dst, send, recv, device):
        return pltpu.make_async_remote_copy(
            src_ref=src, dst_ref=dst, send_sem=send, recv_sem=recv,
            device_id=device, device_id_type=MESH,
        )

    y_dev, k_dev, x_dev = (r, col_of(z, 1 - y, core)), (r, col_of(z, y, 1 - core)), (1 - r, c)
    late = []

    def begin(copy):
        copy.start()
        late.append((None, lambda: copy))

    def later(needed, copy):
        @pl.when(needed)
        def _():
            copy().start()

        late.append((needed, copy))

    def slot(j, index):
        return gath.at[j, pl.ds(pl.multiple_of(index * rows, 16), rows), :]

    first_row = (r * n_col + c) * rows
    first_block, last_block = first_row // width, (first_row + rows - 1) // width
    inside = lax.broadcasted_iota(jnp.int32, (rows, width), 0) < (first_block + 1) * width - first_row

    def along(j, step, d, index):
        to = z - step
        piece = lambda: slot(j, index)
        side = (step + 1) // 2

        def copy():
            there = (r, col_of((to + n_z) % n_z, y, core))
            return remote(piece(), piece(), z_s.at[j, side, d], z_r.at[j, side, d], there)

        return jnp.logical_and(to >= 0, to < n_z), copy

    reduced, coupled = [], {}
    loads[0].wait()
    loads[1].wait()
    for j in range(count):
        mask = jnp.where(
            inside,
            pattern[j, first_block].astype(jnp.float32),
            pattern[j, last_block].astype(jnp.float32),
        )
        current = factor[j] * mask
        for m in range(j):
            current = current - dot3(reduced[m], coupled[j, m])
        reduced.append(split(current))
        gath[j, pl.ds(pl.multiple_of(c * rows, 16), rows), :] = current
        if j == 0:
            pl.semaphore_wait(barrier, n_col)
        own = slot(j, c)
        begin(remote(own, own, y_s.at[j, z], y_r.at[j, z], y_dev))
        for step in (-1, 1):
            later(*along(j, step, 1, c))
        begin(remote(own, own, k_s.at[j, y * n_z + z], k_r.at[j, y * n_z + z], k_dev))
        if j == 0:
            loads[2].wait()
            loads[3].wait()
            linked = {}
        if j + 1 < count:
            for m in range(j + 1):
                now = parent[j + 1] == m
                for p in range(m + 1, j + 1):
                    now = jnp.logical_or(now, jnp.logical_and(parent[j + 1] == p, linked[p, m]))
                linked[j + 1, m] = now
                pair = (j + 1) * j // 2 + m
                links[pair] = couple[pair] * jnp.where(now, 1.0, 0.0)
                coupled[j + 1, m] = split(links[pair])

    diagonal = (
        lax.broadcasted_iota(jnp.int32, (width, width), 0)
        == lax.broadcasted_iota(jnp.int32, (width, width), 1)
    )
    for m in range(count):
        inverse[m, m] = jnp.where(diagonal, 1.0, 0.0)
        for j in range(m):
            inverse[m, j] = jnp.zeros((width, width), jnp.float32)
        for j in range(m + 1, count):
            total = links[j * (j - 1) // 2 + m]
            for q in range(m + 1, j):
                total = total + dot3(split(inverse[m, q]), coupled[j, q])
            inverse[m, j] = -total

    for d in range(1, n_z):
        for j in range(count):
            for step in (-1, 1):
                source = z + step * d
                from_z = (source + n_z) % n_z
                index = col_of(from_z, y, core)
                side = (step + 1) // 2
                there = jnp.logical_and(source >= 0, source < n_z)

                def to_y(j=j, index=index, from_z=from_z):
                    piece = slot(j, index)
                    return remote(piece, piece, y_s.at[j, from_z], y_r.at[j, from_z], y_dev)

                def to_core(j=j, index=index, from_z=from_z):
                    piece, at = slot(j, index), y * n_z + from_z
                    return remote(piece, piece, k_s.at[j, at], k_r.at[j, at], k_dev)

                @pl.when(there)
                def _():
                    piece = slot(j, index)
                    remote(piece, piece, z_s.at[j, side, d], z_r.at[j, side, d], k_dev).wait_recv()

                if d + 1 < n_z:
                    further, onward = along(j, step, d + 1, index)
                    later(jnp.logical_and(there, further), onward)
                later(there, to_y)
                later(there, to_core)

    m, h = mine_slab // halves, mine_slab % halves

    def q_of(rr):
        rho = (rr + z) % 2
        return (1 - core) * 3 * rho + core * (2 - rho)

    q_own, q_other = q_of(r), q_of(1 - r)
    j_own, j_other = jnp.minimum(m + q_own, count - 1), jnp.minimum(m + q_other, count - 1)
    half = pl.ds(pl.multiple_of(h * slab, slab), slab)
    piece_sum = jnp.zeros((slab, width), jnp.float32)
    loads[4].wait()
    for q in range(count):
        left = inverse[q, m, :, half].T
        middle = dot3(split(left), split(diag[q]))
        piece_sum = piece_sum + dot3(split(middle), split(inverse[q, j_own]))
    gpart[2] = piece_sum

    loads[5].wait()
    left_anc = split(anc[...].reshape(2 * rows, anc.shape[2]))

    def relay(j):
        for d in range(n_z):
            from_z = behind(d)
            piece, at = slot(j, col_of(from_z, 1 - y, core)), (1 - y) * n_z + from_z
            remote(piece, piece, y_s.at[j, from_z], y_r.at[j, from_z], y_dev).wait_recv()
            begin(remote(piece, piece, k_s.at[j, at], k_r.at[j, at], k_dev))

    def multiply(j):
        for yy in range(2):
            for zz in range(n_z):
                piece, at = slot(j, col_of(zz, yy, 1 - core)), yy * n_z + zz
                remote(piece, piece, k_s.at[j, at], k_r.at[j, at], k_dev).wait_recv()
        ypart[j] = dot3(left_anc, split(gath[j])).reshape(2, rows, width)
        begin(remote(ypart.at[j, 1 - r], xbuf.at[j], x_s.at[j], x_r.at[j], x_dev))

    def scatter(j):
        remote(ypart.at[j, 1 - r], xbuf.at[j], x_s.at[j], x_r.at[j], x_dev).wait_recv()
        total = ypart[j, r] + xbuf[j]
        yown[j] = total
        cols_out[j] = -total
        for part in range(halves):
            s = j * halves + part
            target = (s + 2) % n_chip
            src = yown.at[j, :, pl.ds(part * slab, slab)]
            dst = ysl.at[pl.ds(pl.multiple_of(c * rows, 16), rows), :]

            @pl.when(chip == target)
            def _():
                ysl[pl.ds(pl.multiple_of(c * rows, 16), rows), :] = total[:, part * slab : (part + 1) * slab]

            @pl.when(chip != target)
            def _():
                remote(src, dst, a_s.at[s], a_r.at[chip], (r, 2 * target + core)).start()

    for j in range(count):
        relay(j)
        if j > 0:
            multiply(j - 1)
        if j > 1:
            scatter(j - 2)
    multiply(count - 1)
    scatter(count - 2)
    scatter(count - 1)

    def slab_rows(index):
        return ysl.at[pl.ds(pl.multiple_of(index * rows, 16), rows), :]

    for e in range(n_chip):
        other = (chip + n_chip - e) % n_chip
        piece = slab_rows(2 * other + core)
        if e:
            remote(piece, piece, a_s.at[0], a_r.at[other], k_dev).wait_recv()
        begin(remote(piece, piece, b_s.at[e], b_r.at[e], k_dev))
    for e in range(n_chip):
        other = (chip + n_chip - e) % n_chip
        piece = slab_rows(2 * other + 1 - core)
        remote(piece, piece, b_s.at[e], b_r.at[e], k_dev).wait_recv()
    left = split(ysl[...].T)
    gpart[1] = dot3(left, split(gath[j_other]))
    begin(remote(gpart.at[1], gbuf, g_s, g_r, x_dev))
    gpart[0] = dot3(left, split(gath[j_own])) + gpart[2]
    remote(gpart.at[1], gbuf, g_s, g_r, x_dev).wait_recv()

    def place(rr, zz, yy, kk):
        rho = (rr + zz) % 2
        q = (1 - kk) * 3 * rho + kk * (2 - rho)
        block, part = slab_of(2 * zz + yy) // halves, slab_of(2 * zz + yy) % halves
        j = block + q
        off = (q + 3) // 4
        index = off * (j * (j - 1) // 2 + block) + (1 - off) * (npair + block)
        return j < count, index * 1, part

    def at_piece(where):
        _, index, part = where
        return win_out.at[index, pl.ds(pl.multiple_of(part * slab, slab), slab), :]

    flip_y, flip_x = 1 - 2 * y, 1 - 2 * r
    r1, y1 = r + core * flip_x, y + (1 - core) * flip_y
    r2, y2 = r + (1 - core) * flip_x, y + core * flip_y
    p_dev, q_dev = (r1, col_of(z, y1, core)), (r2, col_of(z, y2, core))
    def send(where, send_sem, recv_sem, device):
        def copy():
            piece = at_piece(where)
            return remote(piece, piece, send_sem, recv_sem, device)

        later(where[0], copy)

    def receive(where, send_sem, recv_sem, device):
        @pl.when(where[0])
        def _():
            piece = at_piece(where)
            remote(piece, piece, send_sem, recv_sem, device).wait_recv()

    mine = place(r, z, y, core)

    @pl.when(mine[0])
    def _():
        win_out[mine[1], pl.ds(pl.multiple_of(mine[2] * slab, slab), slab), :] = gpart[0] + gbuf[...]

    for d in range(1, n_z):
        send(mine, fz_s.at[d], fz_r.at[d], (r, col_of((z + d) % n_z, y, core)))
    for d in range(n_z):
        where = place(r, behind(d), y, core)
        if d:
            receive(where, fz_s.at[d], fz_r.at[d], k_dev)
        send(where, fp_s.at[d], fp_r.at[d], p_dev)
        send(where, fq_s.at[d], fq_r.at[d], q_dev)
        send(where, fk_s.at[d], fk_r.at[d], k_dev)
    for d in range(n_z):
        where = place(r1, behind(d), y1, core)
        receive(where, fp_s.at[d], fp_r.at[d], k_dev)
        send(where, fq_s.at[n_z + d], fq_r.at[n_z + d], q_dev)
        send(where, fk_s.at[n_z + d], fk_r.at[n_z + d], k_dev)
    for side, (rr, yy) in enumerate(((r2, y2), (1 - r, 1 - y))):
        for d in range(n_z):
            where, at = place(rr, behind(d), yy, core), side * n_z + d
            receive(where, fq_s.at[at], fq_r.at[at], k_dev)
            send(where, fk_s.at[2 * n_z + at], fk_r.at[2 * n_z + at], k_dev)
    for side, (rr, yy) in enumerate(((r, y), (r2, y2), (r1, y1), (1 - r, 1 - y))):
        for d in range(n_z):
            where, at = place(rr, behind(d), yy, 1 - core), side * n_z + d
            receive(where, fk_s.at[at], fk_r.at[at], k_dev)

    for s in range(n_chip):
        target = (s + 2) % n_chip

        @pl.when(chip != target)
        def _():
            src = yown.at[s // halves, :, pl.ds((s % halves) * slab, slab)]
            remote(src, slab_rows(c), a_s.at[s], a_r.at[chip], (r, 2 * target + core)).wait_send()
    for needed, copy in late:
        if needed is None:
            copy().wait_send()
        else:
            @pl.when(needed)
            def _():
                copy().wait_send()


def one_kernel(inv_anc, factor_cols, couple, diag_inv, pattern, parent):
    n_col = lax.axis_size("col")
    count, rows, width = factor_cols.shape
    npair = couple.shape[0]
    n_z, n_chip = n_col // 4, n_col // 2
    slab = count * width // n_chip
    vmem, hbm = pl.BlockSpec(memory_space=pltpu.VMEM), pl.BlockSpec(memory_space=pltpu.HBM)
    anc = inv_anc.reshape(-1, rows, inv_anc.shape[3])
    buffer = lambda *shape: pltpu.VMEM(shape, jnp.float32)
    sems = lambda *shape: pltpu.SemaphoreType.DMA(shape)
    twice = lambda *shape: [sems(*shape), sems(*shape)]
    columns, window = pl.pallas_call(
        functools.partial(window_kernel, n_col),
        out_shape=(
            jax.ShapeDtypeStruct((count, rows, width), jnp.float32),
            jax.ShapeDtypeStruct((npair + count, width, width), jnp.float32),
        ),
        in_specs=[hbm] * 6,
        out_specs=(vmem, vmem),
        scratch_shapes=[
            pltpu.SMEM(pattern.shape, jnp.int32),
            pltpu.SMEM(parent.shape, jnp.int32),
            buffer(*anc.shape),
            buffer(*factor_cols.shape),
            buffer(*couple.shape),
            buffer(*diag_inv.shape),
            sems(6),
            buffer(npair, width, width),
            buffer(count, count, width, width),
            buffer(count, n_col * rows, width),
            buffer(count, 2, rows, width),
            buffer(count, rows, width),
            buffer(count, rows, width),
            buffer(n_col * rows, slab),
            buffer(3, slab, width),
            buffer(slab, width),
            *twice(count, 2, n_z),
            *twice(count, n_z),
            *twice(count, 2 * n_z),
            *twice(count),
            *twice(n_chip),
            *twice(n_chip),
            pltpu.SemaphoreType.DMA,
            pltpu.SemaphoreType.DMA,
            *twice(n_z),
            *twice(n_z),
            *twice(2 * n_z),
            *twice(4 * n_z),
        ],
        compiler_params=pltpu.CompilerParams(
            collective_id=0, has_side_effects=True, vmem_limit_bytes=63 << 20
        ),
    )(pattern, parent, anc, factor_cols, couple, diag_inv)
    return columns, window[:npair], window[npair:]


def solution(mesh):
    in_specs = (P(None, "col", None, "row"), P(None, ("row", "col"), None), P(), P(), P(), P())
    out_specs = (P(None, ("row", "col"), None), P(), P())

    def body(inv_anc, factor_cols, couple, diag_inv, pattern, parent):
        count, rows, width = factor_cols.shape
        slab = count * width // (mesh.shape["col"] // 2)
        fits = mesh.shape["row"] == 2 and mesh.shape["col"] == 4 * count
        fits = fits and slab % 128 == 0 and rows % 16 == 0 and rows <= width and count == 4
        run = one_kernel if fits else shards
        return run(inv_anc, factor_cols, couple, diag_inv, pattern, parent)

    return jax.shard_map(body, mesh=mesh, in_specs=in_specs, out_specs=out_specs, check_vma=False)
```

```python
import functools

import jax
import jax.numpy as jnp
from jax import lax
from jax.experimental import pallas as pl
from jax.experimental.pallas import tpu as pltpu
from jax.sharding import PartitionSpec as P

MESH = pl.DeviceIdType.MESH


def product(left, right):
    return jnp.dot(
        left, right, precision=lax.Precision.HIGH, preferred_element_type=jnp.float32
    )


def ancestry(parent):
    linked = {}
    for j in range(parent.shape[0]):
        for m in range(j):
            linked_now = parent[j] == m
            for p in range(m + 1, j):
                linked_now = linked_now | (parent[j] == p) & linked[p, m]
            linked[j, m] = linked_now
    return linked


def couplings(couple, parent):
    linked = ancestry(parent)
    return {
        (j, m): couple[j * (j - 1) // 2 + m] * linked[j, m].astype(jnp.float32)
        for j, m in linked
    }


def inverse_coupling(blocks, count, width):
    inverse = {}
    for m in range(count):
        inverse[m, m] = jnp.eye(width, dtype=jnp.float32)
        for j in range(m + 1, count):
            total = blocks[j, m]
            for q in range(m + 1, j):
                total = total + product(inverse[m, q], blocks[j, q])
            inverse[m, j] = -total
    return inverse


def shards(inv_anc, factor_cols, couple, diag_inv, pattern, parent):
    count, rows_here, width = factor_cols.shape
    col_count, row_count = lax.axis_size("col"), lax.axis_size("row")
    total_width = count * width
    local_block = inv_anc.reshape(inv_anc.shape[0] * inv_anc.shape[2], inv_anc.shape[3])
    first_row = (lax.axis_index("row") * col_count + lax.axis_index("col")) * rows_here
    block_ids = (first_row + jnp.arange(rows_here, dtype=jnp.int32)) // width
    row_mask = jnp.take(pattern, block_ids, axis=1).astype(jnp.float32)
    masked = factor_cols * row_mask[:, :, None]
    blocks = couplings(couple, parent)
    reduced = []
    for j in range(count):
        current = masked[j]
        for m in range(j):
            current = current - product(reduced[m], blocks[j, m])
        reduced.append(current)
    joined = jnp.concatenate(reduced, axis=1)
    gathered = lax.all_gather(joined, "col", axis=0, tiled=True)
    partial_value = product(local_block, gathered)
    summed = lax.psum_scatter(partial_value, "row", scatter_dimension=0, tiled=True)
    columns = jnp.stack([-summed[:, j * width : (j + 1) * width] for j in range(count)])
    inverse = inverse_coupling(blocks, count, width)
    zero = jnp.zeros((width, width), jnp.float32)
    whole = jnp.concatenate(
        [
            jnp.concatenate([inverse.get((m, j), zero) for j in range(count)], axis=1)
            for m in range(count)
        ],
        axis=0,
    )
    slab = total_width // col_count
    own = lax.dynamic_slice_in_dim(whole, lax.axis_index("col") * slab, slab, axis=1)
    weighted = jnp.concatenate(
        [product(own[q * width : (q + 1) * width].T, diag_inv[q]) for q in range(count)],
        axis=1,
    )
    window = product(weighted, whole)
    exchanged = lax.all_to_all(summed, "col", split_axis=1, concat_axis=0, tiled=True)
    slab_rows = lax.psum_scatter(
        product(exchanged.T, gathered), "row", scatter_dimension=0, tiled=True
    )
    part = slab // row_count
    slab_rows = slab_rows + lax.dynamic_slice_in_dim(
        window, lax.axis_index("row") * part, part, axis=0
    )
    full = lax.all_gather(slab_rows, ("col", "row"), axis=0, tiled=True)

    def block(m, j):
        return full[m * width : (m + 1) * width, j * width : (j + 1) * width]

    pairs = jnp.stack([block(m, j) for j in range(count) for m in range(j)])
    diagonal = jnp.stack([block(j, j) for j in range(count)])
    return columns, pairs, diagonal


def split(value):
    high = value.astype(jnp.bfloat16)
    return high, (value - high.astype(jnp.float32)).astype(jnp.bfloat16)


def dot3(left, right):
    (a, b), (c, d) = left, right
    return (
        jnp.dot(a, c, preferred_element_type=jnp.float32)
        + jnp.dot(a, d, preferred_element_type=jnp.float32)
        + jnp.dot(b, c, preferred_element_type=jnp.float32)
    )


def window_kernel(
    n_col, pattern_in, parent_in, anc_in, factor_in, couple_in, diag_in, cols_out, win_out,
    pattern, parent, anc, factor, couple, diag, in_s, links, inverse, gath, ypart, xbuf, yown, ysl, gpart, gbuf,
    z_s, z_r, y_s, y_r, k_s, k_r, x_s, x_r, a_s, a_r, b_s, b_r, g_s, g_r,
    fz_s, fz_r, fp_s, fp_r, fq_s, fq_r, fk_s, fk_r,
):
    count, rows, width = factor.shape
    n_z, n_chip, slab = n_col // 4, n_col // 2, ysl.shape[1]
    halves = width // slab
    npair = couple.shape[0]
    r, c = lax.axis_index("row"), lax.axis_index("col")
    core, chip = c % 2, c // 2
    y, z = chip % 2, chip // 2

    def col_of(zz, yy, kk):
        return (zz * 2 + yy) * 2 + kk

    def behind(d):
        return (z + n_z - d) % n_z

    def slab_of(cc):
        return (cc + n_chip - 2) % n_chip

    mine_slab = slab_of(chip)

    loads = [
        pltpu.make_async_copy(src, dst, in_s.at[i])
        for i, (src, dst) in enumerate(
            (
                (factor_in, factor), (pattern_in, pattern), (parent_in, parent),
                (couple_in, couple), (diag_in, diag), (anc_in, anc),
            )
        )
    ]
    for load in loads:
        load.start()
    barrier = pltpu.get_barrier_semaphore()
    for e in range(1, n_col):
        pl.semaphore_signal(barrier, inc=1, device_id=(r, (c + e) % n_col), device_id_type=MESH)
    pl.semaphore_signal(barrier, inc=1, device_id=(1 - r, c), device_id_type=MESH)

    def remote(src, dst, send, recv, device):
        return pltpu.make_async_remote_copy(
            src_ref=src, dst_ref=dst, send_sem=send, recv_sem=recv,
            device_id=device, device_id_type=MESH,
        )

    y_dev, k_dev, x_dev = (r, col_of(z, 1 - y, core)), (r, col_of(z, y, 1 - core)), (1 - r, c)
    late = []

    def begin(copy):
        copy.start()
        late.append((None, lambda: copy))

    def later(needed, copy):
        @pl.when(needed)
        def _():
            copy().start()

        late.append((needed, copy))

    def slot(j, index):
        return gath.at[j, pl.ds(pl.multiple_of(index * rows, 16), rows), :]

    first_row = (r * n_col + c) * rows
    first_block, last_block = first_row // width, (first_row + rows - 1) // width
    inside = lax.broadcasted_iota(jnp.int32, (rows, width), 0) < (first_block + 1) * width - first_row

    def along(j, step, d, index):
        to = z - step
        piece = lambda: slot(j, index)
        side = (step + 1) // 2

        def copy():
            there = (r, col_of((to + n_z) % n_z, y, core))
            return remote(piece(), piece(), z_s.at[j, side, d], z_r.at[j, side, d], there)

        return jnp.logical_and(to >= 0, to < n_z), copy

    reduced, coupled = [], {}
    loads[0].wait()
    loads[1].wait()
    for j in range(count):
        mask = jnp.where(
            inside,
            pattern[j, first_block].astype(jnp.float32),
            pattern[j, last_block].astype(jnp.float32),
        )
        current = factor[j] * mask
        for m in range(j):
            current = current - dot3(reduced[m], coupled[j, m])
        reduced.append(split(current))
        gath[j, pl.ds(pl.multiple_of(c * rows, 16), rows), :] = current
        if j == 0:
            pl.semaphore_wait(barrier, n_col)
        own = slot(j, c)
        begin(remote(own, own, y_s.at[j, z], y_r.at[j, z], y_dev))
        for step in (-1, 1):
            later(*along(j, step, 1, c))
        begin(remote(own, own, k_s.at[j, y * n_z + z], k_r.at[j, y * n_z + z], k_dev))
        if j == 0:
            loads[2].wait()
            loads[3].wait()
            linked = {}
        if j + 1 < count:
            for m in range(j + 1):
                now = parent[j + 1] == m
                for p in range(m + 1, j + 1):
                    now = jnp.logical_or(now, jnp.logical_and(parent[j + 1] == p, linked[p, m]))
                linked[j + 1, m] = now
                pair = (j + 1) * j // 2 + m
                links[pair] = couple[pair] * jnp.where(now, 1.0, 0.0)
                coupled[j + 1, m] = split(links[pair])

    for d in range(1, n_z):
        for j in range(count):
            for step in (-1, 1):
                source = z + step * d
                from_z = (source + n_z) % n_z
                index = col_of(from_z, y, core)
                side = (step + 1) // 2
                there = jnp.logical_and(source >= 0, source < n_z)

                def to_y(j=j, index=index, from_z=from_z):
                    piece = slot(j, index)
                    return remote(piece, piece, y_s.at[j, from_z], y_r.at[j, from_z], y_dev)

                def to_core(j=j, index=index, from_z=from_z):
                    piece, at = slot(j, index), y * n_z + from_z
                    return remote(piece, piece, k_s.at[j, at], k_r.at[j, at], k_dev)

                @pl.when(there)
                def _():
                    piece = slot(j, index)
                    remote(piece, piece, z_s.at[j, side, d], z_r.at[j, side, d], k_dev).wait_recv()

                later(there, to_y)
                if d + 1 < n_z:
                    further, onward = along(j, step, d + 1, index)
                    later(jnp.logical_and(there, further), onward)
                later(there, to_core)

    diagonal = (
        lax.broadcasted_iota(jnp.int32, (width, width), 0)
        == lax.broadcasted_iota(jnp.int32, (width, width), 1)
    )
    for m in range(count):
        inverse[m, m] = jnp.where(diagonal, 1.0, 0.0)
        for j in range(m):
            inverse[m, j] = jnp.zeros((width, width), jnp.float32)
        for j in range(m + 1, count):
            total = links[j * (j - 1) // 2 + m]
            for q in range(m + 1, j):
                total = total + dot3(split(inverse[m, q]), coupled[j, q])
            inverse[m, j] = -total

    m, h = mine_slab // halves, mine_slab % halves

    def q_of(rr):
        rho = (rr + z) % 2
        return (1 - core) * 3 * rho + core * (2 - rho)

    q_own, q_other = q_of(r), q_of(1 - r)
    j_own, j_other = jnp.minimum(m + q_own, count - 1), jnp.minimum(m + q_other, count - 1)
    half = pl.ds(pl.multiple_of(h * slab, slab), slab)
    piece_sum = jnp.zeros((slab, width), jnp.float32)
    loads[4].wait()
    for q in range(count):
        left = inverse[q, m, :, half].T
        middle = dot3(split(left), split(diag[q]))
        piece_sum = piece_sum + dot3(split(middle), split(inverse[q, j_own]))
    gpart[2] = piece_sum

    loads[5].wait()
    left_anc = split(anc[...].reshape(2 * rows, anc.shape[2]))

    def relay(j):
        for d in range(n_z):
            from_z = behind(d)
            piece, at = slot(j, col_of(from_z, 1 - y, core)), (1 - y) * n_z + from_z
            remote(piece, piece, y_s.at[j, from_z], y_r.at[j, from_z], y_dev).wait_recv()
            begin(remote(piece, piece, k_s.at[j, at], k_r.at[j, at], k_dev))

    def multiply(j):
        for yy in range(2):
            for zz in range(n_z):
                piece, at = slot(j, col_of(zz, yy, 1 - core)), yy * n_z + zz
                remote(piece, piece, k_s.at[j, at], k_r.at[j, at], k_dev).wait_recv()
        ypart[j] = dot3(left_anc, split(gath[j])).reshape(2, rows, width)
        begin(remote(ypart.at[j, 1 - r], xbuf.at[j], x_s.at[j], x_r.at[j], x_dev))

    def scatter(j):
        remote(ypart.at[j, 1 - r], xbuf.at[j], x_s.at[j], x_r.at[j], x_dev).wait_recv()
        total = ypart[j, r] + xbuf[j]
        yown[j] = total
        cols_out[j] = -total
        for part in range(halves):
            s = j * halves + part
            target = (s + 2) % n_chip
            src = yown.at[j, :, pl.ds(part * slab, slab)]
            dst = ysl.at[pl.ds(pl.multiple_of(c * rows, 16), rows), :]

            @pl.when(chip == target)
            def _():
                ysl[pl.ds(pl.multiple_of(c * rows, 16), rows), :] = total[:, part * slab : (part + 1) * slab]

            @pl.when(chip != target)
            def _():
                remote(src, dst, a_s.at[s], a_r.at[chip], (r, 2 * target + core)).start()

    for j in range(count):
        relay(j)
        if j > 0:
            multiply(j - 1)
        if j > 1:
            scatter(j - 2)
    multiply(count - 1)
    scatter(count - 2)
    scatter(count - 1)

    def slab_rows(index):
        return ysl.at[pl.ds(pl.multiple_of(index * rows, 16), rows), :]

    for e in range(n_chip):
        other = (chip + n_chip - e) % n_chip
        piece = slab_rows(2 * other + core)
        if e:
            remote(piece, piece, a_s.at[0], a_r.at[other], k_dev).wait_recv()
        begin(remote(piece, piece, b_s.at[e], b_r.at[e], k_dev))
    for e in range(n_chip):
        other = (chip + n_chip - e) % n_chip
        piece = slab_rows(2 * other + 1 - core)
        remote(piece, piece, b_s.at[e], b_r.at[e], k_dev).wait_recv()
    left = split(ysl[...].T)
    gpart[1] = dot3(left, split(gath[j_other]))
    begin(remote(gpart.at[1], gbuf, g_s, g_r, x_dev))
    gpart[0] = dot3(left, split(gath[j_own])) + gpart[2]
    remote(gpart.at[1], gbuf, g_s, g_r, x_dev).wait_recv()

    def place(rr, zz, yy, kk):
        rho = (rr + zz) % 2
        q = (1 - kk) * 3 * rho + kk * (2 - rho)
        block, part = slab_of(2 * zz + yy) // halves, slab_of(2 * zz + yy) % halves
        j = block + q
        off = (q + 3) // 4
        index = off * (j * (j - 1) // 2 + block) + (1 - off) * (npair + block)
        return j < count, index * 1, part

    def at_piece(where):
        _, index, part = where
        return win_out.at[index, pl.ds(pl.multiple_of(part * slab, slab), slab), :]

    flip_y, flip_x = 1 - 2 * y, 1 - 2 * r
    r1, y1 = r + core * flip_x, y + (1 - core) * flip_y
    r2, y2 = r + (1 - core) * flip_x, y + core * flip_y
    p_dev, q_dev = (r1, col_of(z, y1, core)), (r2, col_of(z, y2, core))
    def send(where, send_sem, recv_sem, device):
        def copy():
            piece = at_piece(where)
            return remote(piece, piece, send_sem, recv_sem, device)

        later(where[0], copy)

    def receive(where, send_sem, recv_sem, device):
        @pl.when(where[0])
        def _():
            piece = at_piece(where)
            remote(piece, piece, send_sem, recv_sem, device).wait_recv()

    mine = place(r, z, y, core)

    @pl.when(mine[0])
    def _():
        win_out[mine[1], pl.ds(pl.multiple_of(mine[2] * slab, slab), slab), :] = gpart[0] + gbuf[...]

    for d in range(1, n_z):
        send(mine, fz_s.at[d], fz_r.at[d], (r, col_of((z + d) % n_z, y, core)))
    for d in range(n_z):
        where = place(r, behind(d), y, core)
        if d:
            receive(where, fz_s.at[d], fz_r.at[d], k_dev)
        send(where, fp_s.at[d], fp_r.at[d], p_dev)
        send(where, fq_s.at[d], fq_r.at[d], q_dev)
        send(where, fk_s.at[d], fk_r.at[d], k_dev)
    for d in range(n_z):
        where = place(r1, behind(d), y1, core)
        receive(where, fp_s.at[d], fp_r.at[d], k_dev)
        send(where, fq_s.at[n_z + d], fq_r.at[n_z + d], q_dev)
        send(where, fk_s.at[n_z + d], fk_r.at[n_z + d], k_dev)
    for side, (rr, yy) in enumerate(((r2, y2), (1 - r, 1 - y))):
        for d in range(n_z):
            where, at = place(rr, behind(d), yy, core), side * n_z + d
            receive(where, fq_s.at[at], fq_r.at[at], k_dev)
            send(where, fk_s.at[2 * n_z + at], fk_r.at[2 * n_z + at], k_dev)
    for side, (rr, yy) in enumerate(((r, y), (r2, y2), (r1, y1), (1 - r, 1 - y))):
        for d in range(n_z):
            where, at = place(rr, behind(d), yy, 1 - core), side * n_z + d
            receive(where, fk_s.at[at], fk_r.at[at], k_dev)

    for s in range(n_chip):
        target = (s + 2) % n_chip

        @pl.when(chip != target)
        def _():
            src = yown.at[s // halves, :, pl.ds((s % halves) * slab, slab)]
            remote(src, slab_rows(c), a_s.at[s], a_r.at[chip], (r, 2 * target + core)).wait_send()
    for needed, copy in late:
        if needed is None:
            copy().wait_send()
        else:
            @pl.when(needed)
            def _():
                copy().wait_send()


def one_kernel(inv_anc, factor_cols, couple, diag_inv, pattern, parent):
    n_col = lax.axis_size("col")
    count, rows, width = factor_cols.shape
    npair = couple.shape[0]
    n_z, n_chip = n_col // 4, n_col // 2
    slab = count * width // n_chip
    vmem, hbm = pl.BlockSpec(memory_space=pltpu.VMEM), pl.BlockSpec(memory_space=pltpu.HBM)
    anc = inv_anc.reshape(-1, rows, inv_anc.shape[3])
    buffer = lambda *shape: pltpu.VMEM(shape, jnp.float32)
    sems = lambda *shape: pltpu.SemaphoreType.DMA(shape)
    twice = lambda *shape: [sems(*shape), sems(*shape)]
    columns, window = pl.pallas_call(
        functools.partial(window_kernel, n_col),
        out_shape=(
            jax.ShapeDtypeStruct((count, rows, width), jnp.float32),
            jax.ShapeDtypeStruct((npair + count, width, width), jnp.float32),
        ),
        in_specs=[hbm] * 6,
        out_specs=(vmem, vmem),
        scratch_shapes=[
            pltpu.SMEM(pattern.shape, jnp.int32),
            pltpu.SMEM(parent.shape, jnp.int32),
            buffer(*anc.shape),
            buffer(*factor_cols.shape),
            buffer(*couple.shape),
            buffer(*diag_inv.shape),
            sems(6),
            buffer(npair, width, width),
            buffer(count, count, width, width),
            buffer(count, n_col * rows, width),
            buffer(count, 2, rows, width),
            buffer(count, rows, width),
            buffer(count, rows, width),
            buffer(n_col * rows, slab),
            buffer(3, slab, width),
            buffer(slab, width),
            *twice(count, 2, n_z),
            *twice(count, n_z),
            *twice(count, 2 * n_z),
            *twice(count),
            *twice(n_chip),
            *twice(n_chip),
            pltpu.SemaphoreType.DMA,
            pltpu.SemaphoreType.DMA,
            *twice(n_z),
            *twice(n_z),
            *twice(2 * n_z),
            *twice(4 * n_z),
        ],
        compiler_params=pltpu.CompilerParams(
            collective_id=0, has_side_effects=True, vmem_limit_bytes=63 << 20
        ),
    )(pattern, parent, anc, factor_cols, couple, diag_inv)
    return columns, window[:npair], window[npair:]


def solution(mesh):
    in_specs = (P(None, "col", None, "row"), P(None, ("row", "col"), None), P(), P(), P(), P())
    out_specs = (P(None, ("row", "col"), None), P(), P())

    def body(inv_anc, factor_cols, couple, diag_inv, pattern, parent):
        count, rows, width = factor_cols.shape
        slab = count * width // (mesh.shape["col"] // 2)
        fits = mesh.shape["row"] == 2 and mesh.shape["col"] == 4 * count
        fits = fits and slab % 128 == 0 and rows % 16 == 0 and rows <= width and count == 4
        run = one_kernel if fits else shards
        return run(inv_anc, factor_cols, couple, diag_inv, pattern, parent)

    return jax.shard_map(body, mesh=mesh, in_specs=in_specs, out_specs=out_specs, check_vma=False)
```
